128 devices in a mesh: stretch: 4 (over z_lo, core), mp: 32 (over x, y, z_hi).
Axes of the slice: x: 4, y: 4, z: 4 (z_hi: 2, z_lo: 2; z = z_hi * 2 + z_lo), core: 2. Of those that a mesh axis runs over, the one named last changes fastest.
Arguments:
- states: bfloat16 [4, 4096, 3072], P('stretch', 'mp'), may hold values from -6 to 6
- queries: bfloat16 [4, 4096, 1536], P('stretch', 'mp'), may hold values from -32 to 32
- keys: bfloat16 [4, 4096, 512], P('stretch', 'mp'), may hold values from -6 to 6
- values: bfloat16 [4, 4096, 512], P('stretch', 'mp'), may hold values from -6 to 6
- out_weight: bfloat16 [1536, 3072], replicated, may hold values from -0.15625 to 0.15625
- norm_gain: float32 [3072], replicated, may hold values from 0.1 to 1.9
- gate_table: float32 [64, 3072], replicated, may hold values from 0.5 to 1.5
- noise_steps: int32 [4], P('stretch'), may hold values from 0 to 63, as said below
- block_order: int32 [4], replicated, may hold values from 0 to 31, as said below
Outputs:
- mixed: bfloat16 [4, 4096, 3072], P('stretch', 'mp')
The draws below stay inside these ranges and needn't reach their ends.
Inputs may be any that keep to these rules, and one draw needn't show every extreme that they name: `noise_steps`: the latent blocks are at distinct noise levels. `block_order`: distinct positions; only their order matters.
All inputs are finite; a program needn't handle non-finite values.
Results may differ from the reference program's by a relative error of at most 0.011.
Values may be sent and summed in bfloat16 or wider, within the bound.
A program may use at most 128 MiB of HBM per device.

```python
import math
import jax
import jax.numpy as jnp
from jax import lax

D = 3072
HEAD_SIZE = 128
QUERY_HEAD_COUNT = 12
KEY_VALUE_HEADS = 4
STEPS = 64
JOINT_BLOCKS = 4
TOKENS_PER_BLOCK = 4096


def spread_with_ends(key, highest):
    inner_key, place_key = jax.random.split(key)
    inner = jax.random.permutation(inner_key, highest - 1)[:JOINT_BLOCKS - 2] + 1
    joined = jnp.concatenate([jnp.array([0, highest], jnp.int32), inner.astype(jnp.int32)])
    placing = jax.random.permutation(place_key, JOINT_BLOCKS)
    return joined[placing].astype(jnp.int32)


def draw_keys(key, part):
    key = jax.random.fold_in(key, 3)
    starting_block = jnp.clip(jax.random.normal(key, (JOINT_BLOCKS, TOKENS_PER_BLOCK, KEY_VALUE_HEADS * HEAD_SIZE), jnp.float32), -6.0, 6.0)
    return starting_block.astype(jnp.bfloat16)


def draw_queries(key, part):
    key = jax.random.fold_in(key, 5)
    starting_block = jnp.clip(jax.random.normal(key, (JOINT_BLOCKS, TOKENS_PER_BLOCK, QUERY_HEAD_COUNT * HEAD_SIZE), jnp.float32), -6.0, 6.0)
    return starting_block.astype(jnp.bfloat16)


def draw_noise_steps(key, part):
    key = jax.random.fold_in(key, 11)
    return spread_with_ends(key, STEPS - 1)


def draw_block_order(key, part):
    key = jax.random.fold_in(key, 13)
    return spread_with_ends(key, 8 * JOINT_BLOCKS - 1)


def shard_levels(stream_key, extent, shards, least, largest):
    def one(dim, parts):
        draws = jax.random.uniform(jax.random.fold_in(jax.random.fold_in(stream_key, 6), dim), (parts,), jnp.float32, least / len(shards), largest / len(shards))
        return jnp.repeat(jnp.exp(draws), extent[dim] // parts).reshape((-1,) + (1,) * (len(extent) - dim - 1))

    factor_of = one(*shards[0])
    for cut in shards[1:]:
        factor_of = factor_of * one(*cut)
    return factor_of


def centred(stream_key, shape, spread, most, shards=(), held_as=jnp.bfloat16):
    values = jax.random.normal(stream_key, shape, jnp.float32) * spread
    if len(shards) > 0:
        values = shard_levels(stream_key, shape, shards, -0.22, 0.18) * values
    return jnp.clip(values, min=-most, max=most).astype(held_as)


def setup_inputs(seed: int = 0) -> dict:
    key_list = jax.random.split(jax.random.key(seed), 10)
    states = centred(key_list[0], (JOINT_BLOCKS, TOKENS_PER_BLOCK, D), 1.0, 6.0, ((0, 4), (1, 32)))
    queries = draw_queries(jax.random.fold_in(key_list[9], 71), 0)
    keys = draw_keys(jax.random.fold_in(key_list[9], 71), 0)
    values = centred(key_list[3], (JOINT_BLOCKS, TOKENS_PER_BLOCK, KEY_VALUE_HEADS * HEAD_SIZE), 1.0, 6.0, ((0, 4), (1, 32)))
    out_weight = centred(key_list[4], (QUERY_HEAD_COUNT * HEAD_SIZE, D), (QUERY_HEAD_COUNT * HEAD_SIZE) ** -0.5, 0.15625)
    norm_gain = jnp.clip(1.0 + 0.18 * jax.random.normal(key_list[5], (D,), jnp.float32), 0.1, 1.9)
    gate_table = jnp.clip(jax.random.uniform(key_list[6], (STEPS, D), jnp.float32, 0.5, 1.5), 0.5, 1.5)
    noise_steps = draw_noise_steps(jax.random.fold_in(key_list[9], 71), 0)
    block_order = draw_block_order(jax.random.fold_in(key_list[9], 71), 0)
    return dict(states=states, queries=queries, keys=keys, values=values, out_weight=out_weight, norm_gain=norm_gain, gate_table=gate_table, noise_steps=noise_steps, block_order=block_order)


def reference(states, queries, keys, values, out_weight, norm_gain, gate_table, noise_steps, block_order):
    head_groups = QUERY_HEAD_COUNT // KEY_VALUE_HEADS
    scale = 1.0 / math.sqrt(HEAD_SIZE)
    every_key = keys.reshape(JOINT_BLOCKS * TOKENS_PER_BLOCK, KEY_VALUE_HEADS, HEAD_SIZE).astype(jnp.float32)
    every_value = values.reshape(JOINT_BLOCKS * TOKENS_PER_BLOCK, KEY_VALUE_HEADS, HEAD_SIZE).astype(jnp.float32)
    owner = (jnp.arange(JOINT_BLOCKS * TOKENS_PER_BLOCK) // TOKENS_PER_BLOCK).astype(jnp.int32)
    query_row_count = math.gcd(TOKENS_PER_BLOCK, 256)
    results = []
    for block_index in range(JOINT_BLOCKS):
        visible = block_order[owner] <= block_order[block_index]
        query_block_list = queries[block_index].astype(jnp.float32).reshape(TOKENS_PER_BLOCK // query_row_count, query_row_count, KEY_VALUE_HEADS, head_groups, HEAD_SIZE)

        def attend(query_block, visible=visible):
            scores = jnp.einsum('tkgd,nkd->kgtn', query_block, every_key) * scale
            scores = jnp.where(visible, scores, -1e+30)
            top = lax.optimization_barrier(jnp.max(scores, axis=3, keepdims=True))
            weights = jnp.where(visible, jnp.exp(scores - top), 0.0)
            total = lax.optimization_barrier(jnp.sum(weights, axis=3))
            rounded = lax.optimization_barrier(weights.astype(jnp.bfloat16)).astype(jnp.float32)
            summed = jnp.einsum('kgtn,nkd->kgtd', rounded, every_value)
            heads = summed / total[..., None]
            return heads.transpose(2, 0, 1, 3).reshape(query_row_count, QUERY_HEAD_COUNT * HEAD_SIZE).astype(jnp.bfloat16)
        attended = lax.map(attend, query_block_list).reshape(TOKENS_PER_BLOCK, QUERY_HEAD_COUNT * HEAD_SIZE)
        projected = jnp.dot(attended, out_weight, preferred_element_type=jnp.float32)
        normed = projected * lax.rsqrt(lax.optimization_barrier(jnp.mean(projected * projected, axis=-1, keepdims=True)) + 1e-06) * norm_gain
        gate = gate_table[noise_steps[block_index]]
        results.append((states[block_index].astype(jnp.float32) + gate * normed).astype(jnp.bfloat16))
    return jnp.stack(results)
```

```python
import functools
import math

import jax
import jax.numpy as jnp
from jax import lax
from jax.experimental import pallas as pl
from jax.experimental.pallas import tpu as pltpu
from jax.sharding import PartitionSpec as P

HEAD = 128
KV_HEADS = 4
GROUP = 3
WIDE = GROUP * HEAD
TOKENS = 128
BLOCKS = 4
D = 3072
QROWS = BLOCKS * WIDE
SCALE = math.log2(math.e) / math.sqrt(HEAD)
MESH = pl.DeviceIdType.MESH
NT = (((1,), (1,)), ((), ()))

STEPS = (
    ("o00", "s00", "o10", "o20"),
    ("s10", "s20", "o01", "o02"),
    ("s01", "s02", "o30", "o11"),
    ("s30", "s11", "o12", "o21"),
    ("s12", "s21", "o22", "o03"),
    ("s22", "s03", "o13", "o23"),
    ("s13", "s23", "o31", "o32"),
    ("s31", "s32", "o33", "s33"),
)
PLACE = {name: i for i, name in enumerate(n for step in STEPS for n in step)}
HALVES = 4
STEP_ROWS = HALVES * TOKENS


def unit_number(name):
    return int(name[1]) * 4 + int(name[2])


def kernel(
    order_ref, noise_ref, q_hbm, k_hbm, v_hbm, states_hbm, w_hbm, gain_ref, gate_hbm,
    out_ref,
    q_in, k_in, v_in, q_two, kv, scores, top, accum, o_out, o_in, w_v, states_v, gate_v, proj,
    qkv_send, qkv_recv, own_recv, sib_recv, own_send, sib_send, o_send, o_recv, fetch_sem,
):
    st = lax.axis_index("stretch")
    mp = lax.axis_index("mp")
    core = lax.rem(st, 2)
    z_hi = lax.rem(mp, 2)
    z = z_hi * 2 + lax.div(st, 2)
    y = lax.rem(lax.div(mp, 2), 4)
    x = lax.div(mp, 8)

    def device(xx, yy, zz, cc):
        return (lax.rem(zz, 2) * 2 + cc, xx * 8 + yy * 2 + lax.div(zz, 2))

    def ring(axis_is_x, by):
        return device(
            lax.rem(x + by * axis_is_x, 4), lax.rem(y + by * (1 - axis_is_x), 4), z, core
        )

    first_is_x = 1 - core
    first_plus, first_minus = ring(first_is_x, 1), ring(first_is_x, 3)
    second_plus, second_minus = ring(core, 1), ring(core, 3)
    sibling = device(x, y, z, 1 - core)

    barrier = pltpu.get_barrier_semaphore()
    for by in range(1, 8):
        other = lax.rem(z * 2 + core + by, 8)
        pl.semaphore_signal(
            barrier, inc=1, device_id=device(x, y, lax.div(other, 2), lax.rem(other, 2)),
            device_id_type=MESH,
        )
    for neighbour in (first_plus, first_minus, second_plus, second_minus):
        pl.semaphore_signal(barrier, inc=1, device_id=neighbour, device_id_type=MESH)
    pl.semaphore_wait(barrier, 11)

    def spread(by, what, near=False):
        h = lax.rem(z + by, 4)
        source, target, width = ((k_hbm, k_in, HEAD), (v_hbm, v_in, HEAD), (q_hbm, q_in, WIDE))[what]
        src = source.at[0, :, pl.ds(pl.multiple_of(h * width, width), width)]
        if near:
            return pltpu.make_async_copy(src, target.at[st], qkv_recv.at[what, st])
        return pltpu.make_async_remote_copy(
            src_ref=src, dst_ref=target.at[st], send_sem=qkv_send.at[what, by],
            recv_sem=qkv_recv.at[what, st], device_id=device(x, y, h, z_hi), device_id_type=MESH,
        )

    stays = core == z_hi
    for what in range(3):
        for by in (2, 1, 3):
            spread(by, what).start()

        @pl.when(stays)
        def _(what=what):
            spread(0, what, True).start()

        @pl.when(jnp.logical_not(stays))
        def _(what=what):
            spread(0, what).start()

    fetches = [
        pltpu.make_async_copy(w_hbm, w_v, fetch_sem.at[0]),
        pltpu.make_async_copy(gate_hbm, gate_v, fetch_sem.at[1]),
        pltpu.make_async_copy(states_hbm, states_v, fetch_sem.at[2]),
    ]
    for fetch in fetches:
        fetch.start()

    def rank_of(b):
        rank, place = jnp.int32(0), order_ref[b]
        for c in range(BLOCKS):
            other = order_ref[c]
            before = (other < place) | ((other == place) & (c < b))
            rank = rank + jnp.where(before, 1, 0)
        return rank

    ranks = [rank_of(jnp.int32(b)) for b in range(BLOCKS)]
    placed = []
    for i in range(BLOCKS):
        at = jnp.int32(0)
        for b in range(BLOCKS):
            at = at + jnp.where(ranks[b] == i, b, 0)
        placed.append(at)

    def landed(what):
        target = (k_in, v_in, q_in)[what]
        for b in range(BLOCKS):
            pltpu.make_async_copy(target.at[b], target.at[b], qkv_recv.at[what, b]).wait()

    def unit(name):
        return kv.at[PLACE[name]]

    def send(number, source, target, sem, to, part=None):
        src, dst = unit(source), unit(target)
        if part is not None:
            src, dst = src.at[part], dst.at[part]
        return pltpu.make_async_remote_copy(
            src_ref=src, dst_ref=dst, send_sem=own_send.at[number], recv_sem=sem,
            device_id=to, device_id_type=MESH,
        )

    def recv_sem(name, part=0):
        return own_recv.at[unit_number(name), part]

    def first_copies():
        return [
            send(0, "o00", "o10", recv_sem("o10"), first_plus),
            send(1, "o00", "o20", recv_sem("o20"), first_minus),
        ]

    def first_forward(side):
        if side == 1:
            return send(2, "o10", "o30", recv_sem("o30", 0), first_plus, 0)
        return send(3, "o20", "o30", recv_sem("o30", 1), first_minus, 1)

    def second_copies(p):
        here = "o%d0" % p
        return [
            send(4 + p * 4, here, "o%d1" % p, recv_sem("o%d1" % p), second_plus),
            send(5 + p * 4, here, "o%d2" % p, recv_sem("o%d2" % p), second_minus),
        ]

    def second_forward(p, side):
        far = "o%d3" % p
        if side == 1:
            return send(6 + p * 4, "o%d1" % p, far, recv_sem(far, 0), second_plus, 0)
        return send(7 + p * 4, "o%d2" % p, far, recv_sem(far, 1), second_minus, 1)

    def share(name):
        number = unit_number(name)
        return pltpu.make_async_remote_copy(
            src_ref=unit(name), dst_ref=unit("s" + name[1:]), send_sem=sib_send.at[number],
            recv_sem=sib_recv.at[number], device_id=sibling, device_id_type=MESH,
        )

    def arrived(name):
        if name[0] == "s":
            pltpu.make_async_copy(unit(name), unit(name), sib_recv.at[unit_number(name)]).wait()
        elif name[1:] == "00":
            pass
        elif "3" in (name[2],) or name[1:] == "30":
            for part in range(2):
                here = unit(name).at[part]
                pltpu.make_async_copy(here, here, recv_sem(name, part)).wait()
        else:
            pltpu.make_async_copy(unit(name), unit(name), recv_sem(name)).wait()

    def take(name):
        arrived(name)
        if name[0] == "s" or name == "o00":
            return
        share(name).start()
        p, s = int(name[1]), int(name[2])
        if s == 0:
            if p in (1, 2):
                first_forward(p).start()
            for copy in second_copies(p):
                copy.start()
        elif s in (1, 2):
            second_forward(p, s).start()

    landed(0)
    landed(1)
    mine = PLACE["o00"]
    for i in range(BLOCKS):
        kv[mine, 0, i] = k_in[placed[i]]
        kv[mine, 1, i] = v_in[placed[i]]
    for copy in first_copies():
        copy.start()
    share("o00").start()
    for copy in second_copies(0):
        copy.start()

    landed(2)
    for i in range(BLOCKS):
        rows = q_in[placed[i]].astype(jnp.float32) * SCALE
        high = rows.astype(jnp.bfloat16)
        low = (rows - high.astype(jnp.float32)).astype(jnp.bfloat16)
        for g in range(GROUP):
            at = i * WIDE + g * HEAD
            q_two[at:at + TOKENS, 0:HEAD] = high[:, g * HEAD:(g + 1) * HEAD]
            q_two[at:at + TOKENS, HEAD:2 * HEAD] = low[:, g * HEAD:(g + 1) * HEAD]

    accum[...] = jnp.zeros_like(accum)
    top[...] = jnp.full_like(top, -1e30)

    def step(g, carry):
        for number, names in enumerate(STEPS):
            @pl.when(g == number)
            def _(names=names):
                for name in names:
                    if name[0] == "o":
                        take(name)
                for name in names:
                    if name[0] == "s":
                        take(name)

        for j in range(BLOCKS):
            keys = jnp.concatenate([kv[g * HALVES + c, 0, j] for c in range(HALVES)], axis=0)
            scores[j, j * WIDE:QROWS] = lax.dot_general(
                q_two[j * WIDE:QROWS], jnp.concatenate([keys, keys], axis=1), NT,
                preferred_element_type=jnp.float32,
            )
        for i in range(BLOCKS):
            rows = slice(i * WIDE, (i + 1) * WIDE)
            old = top[rows]
            most = old
            for j in range(i + 1):
                for t in range(HALVES):
                    most = jnp.maximum(most, scores[j, rows, t * HEAD:(t + 1) * HEAD])
            new = jnp.broadcast_to(jnp.max(most, axis=1, keepdims=True), old.shape)
            top[rows] = new
            fade = jnp.exp2(old - new)
            total = accum[i] * jnp.concatenate([fade, fade], axis=1)
            shift = jnp.concatenate([new] * HALVES, axis=1)
            for j in range(i + 1):
                weights = jnp.exp2(scores[j, rows] - shift).astype(jnp.bfloat16)
                vals = jnp.concatenate([kv[g * HALVES + c, 1, j] for c in range(HALVES)], axis=0)
                vals = jnp.concatenate([vals, jnp.ones_like(vals)], axis=1)
                total = total + jnp.dot(weights, vals, preferred_element_type=jnp.float32)
            accum[i] = total
        return carry

    lax.fori_loop(0, len(STEPS), step, 0)

    def give(by, near=False):
        b = lax.rem(st + by, 4)
        to = device(x, y, core * 2 + lax.div(b, 2), lax.rem(b, 2))
        if near:
            return pltpu.make_async_copy(o_out.at[by], o_in.at[z], o_recv.at[z])
        return pltpu.make_async_remote_copy(
            src_ref=o_out.at[by], dst_ref=o_in.at[z], send_sem=o_send.at[by],
            recv_sem=o_recv.at[z], device_id=to, device_id_type=MESH,
        )

    for by in (2, 1, 3, 0):
        b = lax.rem(st + by, 4)
        block = accum[rank_of(b)]
        heads = (block[:, :HEAD] / block[:, HEAD:]).astype(jnp.bfloat16)
        for g in range(GROUP):
            o_out[by, :, g * HEAD:(g + 1) * HEAD] = heads[g * TOKENS:(g + 1) * TOKENS]
        if by == 0:
            @pl.when(stays)
            def _():
                give(0, True).start()

            @pl.when(jnp.logical_not(stays))
            def _():
                give(0).start()
        else:
            give(by).start()

    for fetch in fetches:
        fetch.wait()
    for h in range(KV_HEADS):
        pltpu.make_async_copy(o_in.at[h], o_in.at[h], o_recv.at[h]).wait()
    attended = jnp.concatenate([o_in[h] for h in range(KV_HEADS)], axis=1)
    squares = jnp.zeros((TOKENS, 1), jnp.float32)
    tile = 512
    for n in range(D // tile):
        part = jnp.dot(
            attended, w_v[:, n * tile:(n + 1) * tile], preferred_element_type=jnp.float32
        )
        proj[:, n * tile:(n + 1) * tile] = part
        squares = squares + jnp.sum(part * part, axis=1, keepdims=True)
    inverse = lax.rsqrt(squares * (1.0 / D) + 1e-06)
    gate = gate_v[pl.ds(noise_ref[0], 1), :] * gain_ref[...]
    out_ref[0] = (
        states_v[0].astype(jnp.float32) + proj[...] * inverse * gate
    ).astype(jnp.bfloat16)

    for what in range(3):
        for by in (1, 2, 3):
            spread(by, what).wait_send()

        @pl.when(jnp.logical_not(stays))
        def _(what=what):
            spread(0, what).wait_send()
    for copy in first_copies() + [first_forward(1), first_forward(2)]:
        copy.wait_send()
    for p in range(4):
        for copy in second_copies(p) + [second_forward(p, 1), second_forward(p, 2)]:
            copy.wait_send()
        for s in range(4):
            share("o%d%d" % (p, s)).wait_send()
    for by in (1, 2, 3):
        give(by).wait_send()

    @pl.when(jnp.logical_not(stays))
    def _():
        give(0).wait_send()


def local(
    states, queries, keys, values, out_weight, norm_gain, gate_table, noise_steps, block_order
):
    hbm = pl.BlockSpec(memory_space=pl.ANY)
    smem = pl.BlockSpec(memory_space=pltpu.SMEM)
    vmem = pl.BlockSpec(memory_space=pltpu.VMEM)
    bf16, f32 = jnp.bfloat16, jnp.float32
    dma = pltpu.SemaphoreType.DMA
    return pl.pallas_call(
        kernel,
        out_shape=jax.ShapeDtypeStruct((1, TOKENS, D), bf16),
        in_specs=[smem, smem, hbm, hbm, hbm, hbm, hbm, vmem, hbm],
        out_specs=vmem,
        scratch_shapes=[
            pltpu.VMEM((BLOCKS, TOKENS, WIDE), bf16),
            pltpu.VMEM((BLOCKS, TOKENS, HEAD), bf16),
            pltpu.VMEM((BLOCKS, TOKENS, HEAD), bf16),
            pltpu.VMEM((QROWS, 2 * HEAD), bf16),
            pltpu.VMEM((32, 2, BLOCKS, TOKENS, HEAD), bf16),
            pltpu.VMEM((BLOCKS, QROWS, STEP_ROWS), f32),
            pltpu.VMEM((QROWS, HEAD), f32),
            pltpu.VMEM((BLOCKS, WIDE, 2 * HEAD), f32),
            pltpu.VMEM((BLOCKS, TOKENS, WIDE), bf16),
            pltpu.VMEM((KV_HEADS, TOKENS, WIDE), bf16),
            pltpu.VMEM((KV_HEADS * WIDE, D), bf16),
            pltpu.VMEM((1, TOKENS, D), bf16),
            pltpu.VMEM(gate_table.shape, f32),
            pltpu.VMEM((TOKENS, D), f32),
            dma((3, 4)), dma((3, 4)), dma((16, 2)), dma((16,)), dma((20,)), dma((16,)),
            dma((4,)), dma((4,)), dma((3,)),
        ],
        compiler_params=pltpu.CompilerParams(
            collective_id=0, has_side_effects=True, vmem_limit_bytes=56 * 2**20
        ),
        cost_estimate=pl.CostEstimate(
            flops=9_300_000_000, bytes_accessed=20_000_000, transcendentals=16_000_000
        ),
        name="attend",
    )(
        block_order, noise_steps, queries, keys, values, states, out_weight,
        norm_gain.reshape(1, D), gate_table,
    )


def solution(mesh):
    placed = (
        P("stretch", "mp", None),
        P("stretch", "mp", None),
        P("stretch", "mp", None),
        P("stretch", "mp", None),
        P(),
        P(),
        P(),
        P("stretch"),
        P(),
    )
    return jax.shard_map(
        local, mesh=mesh, in_specs=placed, out_specs=P("stretch", "mp", None), check_vma=False
    )
```

```python
import functools
import math

import jax
import jax.numpy as jnp
from jax import lax
from jax.experimental import pallas as pl
from jax.experimental.pallas import tpu as pltpu
from jax.sharding import PartitionSpec as P

HEAD = 128
KV_HEADS = 4
GROUP = 3
WIDE = GROUP * HEAD
TOKENS = 128
BLOCKS = 4
D = 3072
QROWS = BLOCKS * WIDE
SCALE = math.log2(math.e) / math.sqrt(HEAD)
MESH = pl.DeviceIdType.MESH
NT = (((1,), (1,)), ((), ()))

STEPS = (
    ("o00", "o20"),
    ("s00", "s10"),
    ("s20", "o10"),
    ("o02", "o01"),
    ("o12", "o11"),
    ("o30", "s01"),
    ("s11", "s02"),
    ("o22", "s12"),
    ("o21", "o03"),
    ("s30", "s21"),
    ("o32", "s22"),
    ("o31", "s03"),
    ("s31", "o13"),
    ("o23", "o33"),
    ("s32", "s23"),
    ("s33", "s13"),
)
SENDS = {
    0: ("S00", "S01"),
    1: ("S11", "S10"),
    2: ("f3",),
    3: ("S20", "S21"),
    4: ("F0",),
    6: ("S31", "S30"),
    7: ("F2",),
    8: ("o03", "F1"),
    10: ("F3",),
    12: ("o23",),
    14: ("o33",),
}
PLACE = {name: i for i, name in enumerate(n for step in STEPS for n in step)}
HALVES = 2
STEP_ROWS = HALVES * TOKENS
FETCH_STEP = 5


def unit_number(name):
    return int(name[1]) * 4 + int(name[2])


def needed(op):
    if op == "f3":
        return ("o10", "o20")
    if op[0] == "S":
        return ("o%s0" % op[1],)
    if op[0] == "F":
        return ("o%s1" % op[1], "o%s2" % op[1])
    return (op,)


def plan():
    taken, steps = {"o00"}, []
    for number, names in enumerate(STEPS):
        todo = []
        for op in SENDS.get(number, ()) + names:
            for name in needed(op):
                if name not in taken:
                    taken.add(name)
                    todo.append(name)
            if op[0] in "fSF":
                todo.append(op)
        steps.append(tuple(todo))
    return steps


def kernel(
    order_ref, noise_ref, q_hbm, k_hbm, v_hbm, states_hbm, w_hbm, gain_ref, gate_hbm,
    out_ref,
    q_in, k_in, v_in, q_two, kv, scores, top, accum, o_out, o_in, w_v, states_v, gate_v, proj,
    qkv_send, qkv_recv, own_recv, sib_recv, own_send, sib_send, o_send, o_recv, fetch_sem,
):
    st = lax.axis_index("stretch")
    mp = lax.axis_index("mp")
    core = lax.rem(st, 2)
    z_hi = lax.rem(mp, 2)
    z = z_hi * 2 + lax.div(st, 2)
    y = lax.rem(lax.div(mp, 2), 4)
    x = lax.div(mp, 8)

    def device(xx, yy, zz, cc):
        return (lax.rem(zz, 2) * 2 + cc, xx * 8 + yy * 2 + lax.div(zz, 2))

    def ring(axis_is_x, by):
        return device(
            lax.rem(x + by * axis_is_x, 4), lax.rem(y + by * (1 - axis_is_x), 4), z, core
        )

    first_is_x = 1 - core
    first_plus, first_minus = ring(first_is_x, 1), ring(first_is_x, 3)
    second_plus, second_minus = ring(core, 1), ring(core, 3)
    sibling = device(x, y, z, 1 - core)

    barrier = pltpu.get_barrier_semaphore()
    for by in range(1, 8):
        other = lax.rem(z * 2 + core + by, 8)
        pl.semaphore_signal(
            barrier, inc=1, device_id=device(x, y, lax.div(other, 2), lax.rem(other, 2)),
            device_id_type=MESH,
        )
    for neighbour in (first_plus, first_minus, second_plus, second_minus):
        pl.semaphore_signal(barrier, inc=1, device_id=neighbour, device_id_type=MESH)
    pl.semaphore_wait(barrier, 11)

    def spread(by, what, near=False):
        h = lax.rem(z + by, 4)
        source, target, width = ((k_hbm, k_in, HEAD), (v_hbm, v_in, HEAD), (q_hbm, q_in, WIDE))[what]
        src = source.at[0, :, pl.ds(pl.multiple_of(h * width, width), width)]
        if near:
            return pltpu.make_async_copy(src, target.at[st], qkv_recv.at[what, st])
        return pltpu.make_async_remote_copy(
            src_ref=src, dst_ref=target.at[st], send_sem=qkv_send.at[what, by],
            recv_sem=qkv_recv.at[what, st], device_id=device(x, y, h, z_hi), device_id_type=MESH,
        )

    stays = core == z_hi
    for what in range(3):
        for by in (2, 1, 3):
            spread(by, what).start()

        @pl.when(stays)
        def _(what=what):
            spread(0, what, True).start()

        @pl.when(jnp.logical_not(stays))
        def _(what=what):
            spread(0, what).start()

    fetches = [
        pltpu.make_async_copy(w_hbm, w_v, fetch_sem.at[0]),
        pltpu.make_async_copy(gate_hbm, gate_v, fetch_sem.at[1]),
        pltpu.make_async_copy(states_hbm, states_v, fetch_sem.at[2]),
    ]
    def rank_of(b):
        rank, place = jnp.int32(0), order_ref[b]
        for c in range(BLOCKS):
            other = order_ref[c]
            before = (other < place) | ((other == place) & (c < b))
            rank = rank + jnp.where(before, 1, 0)
        return rank

    ranks = [rank_of(jnp.int32(b)) for b in range(BLOCKS)]
    placed = []
    for i in range(BLOCKS):
        at = jnp.int32(0)
        for b in range(BLOCKS):
            at = at + jnp.where(ranks[b] == i, b, 0)
        placed.append(at)

    def landed(what):
        target = (k_in, v_in, q_in)[what]
        for b in range(BLOCKS):
            pltpu.make_async_copy(target.at[b], target.at[b], qkv_recv.at[what, b]).wait()

    def unit(name):
        return kv.at[PLACE[name]]

    def send(number, source, target, sem, to, part=None):
        src, dst = unit(source), unit(target)
        if part is not None:
            src, dst = src.at[part], dst.at[part]
        return pltpu.make_async_remote_copy(
            src_ref=src, dst_ref=dst, send_sem=own_send.at[number], recv_sem=sem,
            device_id=to, device_id_type=MESH,
        )

    def recv_sem(name, part=0):
        return own_recv.at[unit_number(name), part]

    def first_copies(part):
        return [
            send(part * 2, "o00", "o10", recv_sem("o10", part), first_plus, part),
            send(part * 2 + 1, "o00", "o20", recv_sem("o20", part), first_minus, part),
        ]

    def first_forwards():
        return [
            send(4, "o10", "o30", recv_sem("o30", 0), first_plus, 0),
            send(5, "o20", "o30", recv_sem("o30", 1), first_minus, 1),
        ]

    def second_copies(p, part):
        here, at = "o%d0" % p, 6 + p * 6 + part * 2
        plus, minus = "o%d1" % p, "o%d2" % p
        return [
            send(at, here, plus, recv_sem(plus, part), second_plus, part),
            send(at + 1, here, minus, recv_sem(minus, part), second_minus, part),
        ]

    def second_forwards(p):
        far, at = "o%d3" % p, 10 + p * 6
        return [
            send(at, "o%d1" % p, far, recv_sem(far, 0), second_plus, 0),
            send(at + 1, "o%d2" % p, far, recv_sem(far, 1), second_minus, 1),
        ]

    def share(name):
        number = unit_number(name)
        return pltpu.make_async_remote_copy(
            src_ref=unit(name), dst_ref=unit("s" + name[1:]), send_sem=sib_send.at[number],
            recv_sem=sib_recv.at[number], device_id=sibling, device_id_type=MESH,
        )

    def begin(copies):
        for copy in copies:
            copy.start()

    def act(op):
        if op == "f3":
            begin(first_forwards())
        elif op[0] == "S":
            begin(second_copies(int(op[1]), int(op[2])))
        elif op[0] == "F":
            begin(second_forwards(int(op[1])))
        elif op[0] == "s":
            pltpu.make_async_copy(unit(op), unit(op), sib_recv.at[unit_number(op)]).wait()
        else:
            for part in range(2):
                here = unit(op).at[part]
                pltpu.make_async_copy(here, here, recv_sem(op, part)).wait()
            share(op).start()

    mine = PLACE["o00"]
    for part, source in ((0, k_in), (1, v_in)):
        landed(part)
        for i in range(BLOCKS):
            kv[mine, part, i] = source[placed[i]]
        begin(first_copies(part))
    share("o00").start()

    landed(2)
    for i in range(BLOCKS):
        rows = q_in[placed[i]].astype(jnp.float32) * SCALE
        high = rows.astype(jnp.bfloat16)
        low = (rows - high.astype(jnp.float32)).astype(jnp.bfloat16)
        for g in range(GROUP):
            at = i * WIDE + g * HEAD
            q_two[at:at + TOKENS, 0:HEAD] = high[:, g * HEAD:(g + 1) * HEAD]
            q_two[at:at + TOKENS, HEAD:2 * HEAD] = low[:, g * HEAD:(g + 1) * HEAD]

    accum[...] = jnp.zeros_like(accum)
    top[...] = jnp.full_like(top, -1e30)

    plans = plan()

    def events(number):
        for op in plans[number]:
            act(op)
        if number == FETCH_STEP:
            for fetch in fetches:
                fetch.start()

    def scored(g, held, j):
        keys = jnp.concatenate([kv[g * HALVES + c, 0, j] for c in range(HALVES)], axis=0)
        scores[held, j, j * WIDE:QROWS] = lax.dot_general(
            q_two[j * WIDE:QROWS], jnp.concatenate([keys, keys], axis=1), NT,
            preferred_element_type=jnp.float32,
        )

    def weighed(g, held, i):
        rows = slice(i * WIDE, (i + 1) * WIDE)
        old = top[rows]
        most = old
        for j in range(i + 1):
            for t in range(HALVES):
                most = jnp.maximum(most, scores[held, j, rows, t * HEAD:(t + 1) * HEAD])
        new = jnp.broadcast_to(jnp.max(most, axis=1, keepdims=True), old.shape)
        top[rows] = new
        fade = jnp.exp2(old - new)
        total = accum[i] * jnp.concatenate([fade, fade], axis=1)
        shift = jnp.concatenate([new] * HALVES, axis=1)
        for j in range(i + 1):
            weights = jnp.exp2(scores[held, j, rows] - shift).astype(jnp.bfloat16)
            vals = jnp.concatenate([kv[g * HALVES + c, 1, j] for c in range(HALVES)], axis=0)
            vals = jnp.concatenate([vals, jnp.ones_like(vals)], axis=1)
            total = total + jnp.dot(weights, vals, preferred_element_type=jnp.float32)
        accum[i] = total

    def pair(g, held):
        for i in range(BLOCKS):
            scored(g + 1, 1 - held, i)
            weighed(g, held, i)

    last = len(STEPS) - 1
    events(0)
    for i in range(BLOCKS):
        scored(0, 0, i)

    for g in range(last):
        events(g + 1)
        pair(g, g % 2)
    for i in range(BLOCKS):
        weighed(last, last % 2, i)

    def give(by, near=False):
        b = lax.rem(st + by, 4)
        to = device(x, y, core * 2 + lax.div(b, 2), lax.rem(b, 2))
        if near:
            return pltpu.make_async_copy(o_out.at[by], o_in.at[z], o_recv.at[z])
        return pltpu.make_async_remote_copy(
            src_ref=o_out.at[by], dst_ref=o_in.at[z], send_sem=o_send.at[by],
            recv_sem=o_recv.at[z], device_id=to, device_id_type=MESH,
        )

    for by in (2, 1, 3, 0):
        b = lax.rem(st + by, 4)
        block = accum[rank_of(b)]
        heads = (block[:, :HEAD] / block[:, HEAD:]).astype(jnp.bfloat16)
        for g in range(GROUP):
            o_out[by, :, g * HEAD:(g + 1) * HEAD] = heads[g * TOKENS:(g + 1) * TOKENS]
        if by == 0:
            @pl.when(stays)
            def _():
                give(0, True).start()

            @pl.when(jnp.logical_not(stays))
            def _():
                give(0).start()
        else:
            give(by).start()

    for what in range(3):
        for by in (1, 2, 3):
            spread(by, what).wait_send()

        @pl.when(jnp.logical_not(stays))
        def _(what=what):
            spread(0, what).wait_send()
    gone = first_copies(0) + first_copies(1) + first_forwards()
    for p in range(4):
        gone += second_copies(p, 0) + second_copies(p, 1) + second_forwards(p)
        gone += [share("o%d%d" % (p, s)) for s in range(4)]
    for copy in gone:
        copy.wait_send()

    for fetch in fetches:
        fetch.wait()
    squares = jnp.zeros((TOKENS, 1), jnp.float32)
    tile = 512
    for number, by in enumerate((0, 1, 3, 2)):
        h = lax.rem(z + by, 4)
        pltpu.make_async_copy(o_in.at[h], o_in.at[h], o_recv.at[h]).wait()
        attended = o_in[h]
        rows = pl.ds(pl.multiple_of(h * WIDE, WIDE), WIDE)
        for n in range(D // tile):
            cols = slice(n * tile, (n + 1) * tile)
            part = jnp.dot(attended, w_v[rows, cols], preferred_element_type=jnp.float32)
            if number > 0:
                part = part + proj[:, cols]
            proj[:, cols] = part
            if number == 3:
                squares = squares + jnp.sum(part * part, axis=1, keepdims=True)
    inverse = lax.rsqrt(squares * (1.0 / D) + 1e-06)
    gate = gate_v[pl.ds(noise_ref[0], 1), :] * gain_ref[...]
    out_ref[0] = (
        states_v[0].astype(jnp.float32) + proj[...] * inverse * gate
    ).astype(jnp.bfloat16)

    for by in (1, 2, 3):
        give(by).wait_send()

    @pl.when(jnp.logical_not(stays))
    def _():
        give(0).wait_send()


def local(
    states, queries, keys, values, out_weight, norm_gain, gate_table, noise_steps, block_order
):
    hbm = pl.BlockSpec(memory_space=pl.ANY)
    smem = pl.BlockSpec(memory_space=pltpu.SMEM)
    vmem = pl.BlockSpec(memory_space=pltpu.VMEM)
    bf16, f32 = jnp.bfloat16, jnp.float32
    dma = pltpu.SemaphoreType.DMA
    return pl.pallas_call(
        kernel,
        out_shape=jax.ShapeDtypeStruct((1, TOKENS, D), bf16),
        in_specs=[smem, smem, hbm, hbm, hbm, hbm, hbm, vmem, hbm],
        out_specs=vmem,
        scratch_shapes=[
            pltpu.VMEM((BLOCKS, TOKENS, WIDE), bf16),
            pltpu.VMEM((BLOCKS, TOKENS, HEAD), bf16),
            pltpu.VMEM((BLOCKS, TOKENS, HEAD), bf16),
            pltpu.VMEM((QROWS, 2 * HEAD), bf16),
            pltpu.VMEM((32, 2, BLOCKS, TOKENS, HEAD), bf16),
            pltpu.VMEM((2, BLOCKS, QROWS, STEP_ROWS), f32),
            pltpu.VMEM((QROWS, HEAD), f32),
            pltpu.VMEM((BLOCKS, WIDE, 2 * HEAD), f32),
            pltpu.VMEM((BLOCKS, TOKENS, WIDE), bf16),
            pltpu.VMEM((KV_HEADS, TOKENS, WIDE), bf16),
            pltpu.VMEM((KV_HEADS * WIDE, D), bf16),
            pltpu.VMEM((1, TOKENS, D), bf16),
            pltpu.VMEM(gate_table.shape, f32),
            pltpu.VMEM((TOKENS, D), f32),
            dma((3, 4)), dma((3, 4)), dma((16, 2)), dma((16,)), dma((30,)), dma((16,)),
            dma((4,)), dma((4,)), dma((3,)),
        ],
        compiler_params=pltpu.CompilerParams(
            collective_id=0, has_side_effects=True, vmem_limit_bytes=56 * 2**20
        ),
        cost_estimate=pl.CostEstimate(
            flops=9_300_000_000, bytes_accessed=20_000_000, transcendentals=16_000_000
        ),
        name="attend",
    )(
        block_order, noise_steps, queries, keys, values, states, out_weight,
        norm_gain.reshape(1, D), gate_table,
    )


def solution(mesh):
    placed = (
        P("stretch", "mp", None),
        P("stretch", "mp", None),
        P("stretch", "mp", None),
        P("stretch", "mp", None),
        P(),
        P(),
        P(),
        P("stretch"),
        P(),
    )
    return jax.shard_map(
        local, mesh=mesh, in_specs=placed, out_specs=P("stretch", "mp", None), check_vma=False
    )
```

```python
import functools
import math

import jax
import jax.numpy as jnp
from jax import lax
from jax.experimental import pallas as pl
from jax.experimental.pallas import tpu as pltpu
from jax.sharding import PartitionSpec as P

HEAD = 128
KV_HEADS = 4
GROUP = 3
WIDE = GROUP * HEAD
TOKENS = 128
BLOCKS = 4
D = 3072
QROWS = BLOCKS * WIDE
SCALE = math.log2(math.e) / math.sqrt(HEAD)
MESH = pl.DeviceIdType.MESH
NT = (((1,), (1,)), ((), ()))

STEPS = (
    ("o00", "s00"),
    ("o20", "o10"),
    ("s10", "s20"),
    ("o02", "o01"),
    ("s02", "s01"),
    ("o12", "o11"),
    ("o30", "s12"),
    ("o03", "s11"),
    ("s30", "o22"),
    ("s21", "o21"),
    ("o32", "s03"),
    ("s31", "o31"),
    ("o23", "s22"),
    ("o13", "s32"),
    ("o33", "s13"),
    ("s23", "s33"),
)
SENDS = {
    1: ("o20", "o10", "S10", "S11", "f3"),
    3: ("o02", "o01", "F0"),
    4: ("S20", "S21"),
    5: ("o30",),
    6: ("S31", "S30"),
    8: ("o21", "F2"),
    9: ("F1",),
    10: ("o31", "F3"),
}
PLACE = {name: i for i, name in enumerate(n for step in STEPS for n in step)}
HALVES = 2
STEP_ROWS = HALVES * TOKENS
FETCH_STEPS = range(2, 2 + KV_HEADS * GROUP)


def unit_number(name):
    return int(name[1]) * 4 + int(name[2])


def needed(op):
    if op == "f3":
        return ("o10", "o20")
    if op[0] == "S":
        return ("o%s0" % op[1],)
    if op[0] == "F":
        return ("o%s1" % op[1], "o%s2" % op[1])
    return (op,)


def plan():
    taken, steps = {"o00"}, []
    for number, names in enumerate(STEPS):
        todo = []
        for op in SENDS.get(number, ()) + names:
            for name in needed(op):
                if name not in taken:
                    taken.add(name)
                    todo.append(name)
            if op[0] in "fSF":
                todo.append(op)
        steps.append(tuple(todo))
    return steps


def kernel(
    order_ref, noise_ref, q_hbm, k_hbm, v_hbm, states_hbm, w_hbm, gain_ref, gate_hbm,
    out_hbm,
    q_in, k_in, v_in, q_two, kv, scores, top, accum, o_out, o_in, w_v, states_v, gate_v, proj, mixed,
    qkv_send, qkv_recv, own_recv, sib_recv, own_send, sib_send, o_send, o_recv, fetch_sem, out_sem,
):
    st = lax.axis_index("stretch")
    mp = lax.axis_index("mp")
    core = lax.rem(st, 2)
    z_hi = lax.rem(mp, 2)
    z = z_hi * 2 + lax.div(st, 2)
    y = lax.rem(lax.div(mp, 2), 4)
    x = lax.div(mp, 8)

    def device(xx, yy, zz, cc):
        return (lax.rem(zz, 2) * 2 + cc, xx * 8 + yy * 2 + lax.div(zz, 2))

    def ring(axis_is_x, by):
        return device(
            lax.rem(x + by * axis_is_x, 4), lax.rem(y + by * (1 - axis_is_x), 4), z, core
        )

    first_is_x = 1 - core
    first_plus, first_minus = ring(first_is_x, 1), ring(first_is_x, 3)
    second_plus, second_minus = ring(core, 1), ring(core, 3)
    sibling = device(x, y, z, 1 - core)

    barrier = pltpu.get_barrier_semaphore()
    for by in range(1, 8):
        other = lax.rem(z * 2 + core + by, 8)
        pl.semaphore_signal(
            barrier, inc=1, device_id=device(x, y, lax.div(other, 2), lax.rem(other, 2)),
            device_id_type=MESH,
        )
    for neighbour in (first_plus, first_minus, second_plus, second_minus):
        pl.semaphore_signal(barrier, inc=1, device_id=neighbour, device_id_type=MESH)
    pl.semaphore_wait(barrier, 11)

    def spread(by, what, near=False):
        h = lax.rem(z + by, 4)
        source, target, width = ((k_hbm, k_in, HEAD), (v_hbm, v_in, HEAD), (q_hbm, q_in, WIDE))[what]
        src = source.at[0, :, pl.ds(pl.multiple_of(h * width, width), width)]
        if near:
            return pltpu.make_async_copy(src, target.at[st], qkv_recv.at[what, st])
        return pltpu.make_async_remote_copy(
            src_ref=src, dst_ref=target.at[st], send_sem=qkv_send.at[what, by],
            recv_sem=qkv_recv.at[what, st], device_id=device(x, y, h, z_hi), device_id_type=MESH,
        )

    stays = core == z_hi
    for what in range(3):
        for by in (2, 1, 3):
            spread(by, what).start()

        @pl.when(stays)
        def _(what=what):
            spread(0, what, True).start()

        @pl.when(jnp.logical_not(stays))
        def _(what=what):
            spread(0, what).start()

    def weights(number):
        rows = slice(number * TOKENS, (number + 1) * TOKENS)
        return pltpu.make_async_copy(w_hbm.at[rows], w_v.at[rows], fetch_sem.at[0])

    fetches = [
        pltpu.make_async_copy(gate_hbm, gate_v, fetch_sem.at[1]),
        pltpu.make_async_copy(states_hbm, states_v, fetch_sem.at[2]),
        pltpu.make_async_copy(w_hbm, w_v, fetch_sem.at[0]),
    ]

    def rank_of(b):
        rank, place = jnp.int32(0), order_ref[b]
        for c in range(BLOCKS):
            other = order_ref[c]
            before = (other < place) | ((other == place) & (c < b))
            rank = rank + jnp.where(before, 1, 0)
        return rank

    ranks = [rank_of(jnp.int32(b)) for b in range(BLOCKS)]
    placed = []
    for i in range(BLOCKS):
        at = jnp.int32(0)
        for b in range(BLOCKS):
            at = at + jnp.where(ranks[b] == i, b, 0)
        placed.append(at)

    def landed(what):
        target = (k_in, v_in, q_in)[what]
        for b in range(BLOCKS):
            pltpu.make_async_copy(target.at[b], target.at[b], qkv_recv.at[what, b]).wait()

    def unit(name):
        return kv.at[PLACE[name]]

    def send(number, source, target, sem, to, part=None):
        src, dst = unit(source), unit(target)
        if part is not None:
            src, dst = src.at[part], dst.at[part]
        return pltpu.make_async_remote_copy(
            src_ref=src, dst_ref=dst, send_sem=own_send.at[number], recv_sem=sem,
            device_id=to, device_id_type=MESH,
        )

    def recv_sem(name, part=0):
        return own_recv.at[unit_number(name), part]

    def first_copies(part):
        return [
            send(part * 2, "o00", "o10", recv_sem("o10", part), first_plus, part),
            send(part * 2 + 1, "o00", "o20", recv_sem("o20", part), first_minus, part),
        ]

    def first_forwards():
        return [
            send(4, "o10", "o30", recv_sem("o30", 0), first_plus, 0),
            send(5, "o20", "o30", recv_sem("o30", 1), first_minus, 1),
        ]

    def second_copies(p, part):
        here, at = "o%d0" % p, 6 + p * 6 + part * 2
        plus, minus = "o%d1" % p, "o%d2" % p
        return [
            send(at, here, plus, recv_sem(plus, part), second_plus, part),
            send(at + 1, here, minus, recv_sem(minus, part), second_minus, part),
        ]

    def second_forwards(p):
        far, at = "o%d3" % p, 10 + p * 6
        return [
            send(at, "o%d1" % p, far, recv_sem(far, 0), second_plus, 0),
            send(at + 1, "o%d2" % p, far, recv_sem(far, 1), second_minus, 1),
        ]

    def share(name):
        number = unit_number(name)
        return pltpu.make_async_remote_copy(
            src_ref=unit(name), dst_ref=unit("s" + name[1:]), send_sem=sib_send.at[number],
            recv_sem=sib_recv.at[number], device_id=sibling, device_id_type=MESH,
        )

    def begin(copies):
        for copy in copies:
            copy.start()

    def act(op):
        if op == "f3":
            begin(first_forwards())
        elif op[0] == "S":
            begin(second_copies(int(op[1]), int(op[2])))
        elif op[0] == "F":
            begin(second_forwards(int(op[1])))
        elif op[0] == "s":
            pltpu.make_async_copy(unit(op), unit(op), sib_recv.at[unit_number(op)]).wait()
        else:
            for part in range(2):
                here = unit(op).at[part]
                pltpu.make_async_copy(here, here, recv_sem(op, part)).wait()
            share(op).start()

    mine = PLACE["o00"]
    for part, source in ((0, k_in), (1, v_in)):
        landed(part)
        for i in range(BLOCKS):
            kv[mine, part, i] = source[placed[i]]
        begin(first_copies(part))
    share("o00").start()

    landed(2)
    begin(second_copies(0, 0) + second_copies(0, 1))
    for i in range(BLOCKS):
        rows = q_in[placed[i]].astype(jnp.float32) * SCALE
        high = rows.astype(jnp.bfloat16)
        low = (rows - high.astype(jnp.float32)).astype(jnp.bfloat16)
        for g in range(GROUP):
            at = i * WIDE + g * HEAD
            q_two[at:at + TOKENS, 0:HEAD] = high[:, g * HEAD:(g + 1) * HEAD]
            q_two[at:at + TOKENS, HEAD:2 * HEAD] = low[:, g * HEAD:(g + 1) * HEAD]

    accum[...] = jnp.zeros_like(accum)
    top[...] = jnp.full_like(top, -1e30)

    plans = plan()

    def events(number):
        for op in plans[number]:
            act(op)
        if number in FETCH_STEPS:
            weights(number - FETCH_STEPS[0]).start()
        if number == FETCH_STEPS[0]:
            fetches[0].start()
            fetches[1].start()

    def scored(g, held, j):
        keys = jnp.concatenate([kv[g * HALVES + c, 0, j] for c in range(HALVES)], axis=0)
        scores[held, j, j * WIDE:QROWS] = lax.dot_general(
            q_two[j * WIDE:QROWS], jnp.concatenate([keys, keys], axis=1), NT,
            preferred_element_type=jnp.float32,
        )

    def weighed(g, held, i):
        rows = slice(i * WIDE, (i + 1) * WIDE)
        old = top[rows]
        most = old
        for j in range(i + 1):
            for t in range(HALVES):
                most = jnp.maximum(most, scores[held, j, rows, t * HEAD:(t + 1) * HEAD])
        new = jnp.broadcast_to(jnp.max(most, axis=1, keepdims=True), old.shape)
        top[rows] = new
        fade = jnp.exp2(old - new)
        total = accum[i] * jnp.concatenate([fade, fade], axis=1)
        shift = jnp.concatenate([new] * HALVES, axis=1)
        for j in range(i + 1):
            weights = jnp.exp2(scores[held, j, rows] - shift).astype(jnp.bfloat16)
            vals = jnp.concatenate([kv[g * HALVES + c, 1, j] for c in range(HALVES)], axis=0)
            vals = jnp.concatenate([vals, jnp.ones_like(vals)], axis=1)
            total = total + jnp.dot(weights, vals, preferred_element_type=jnp.float32)
        accum[i] = total

    def pair(g, held):
        for i in range(BLOCKS):
            scored(g + 1, 1 - held, i)
            weighed(g, held, i)

    last = len(STEPS) - 1
    events(0)
    for i in range(BLOCKS):
        scored(0, 0, i)

    for g in range(last):
        events(g + 1)
        pair(g, g % 2)
    for i in range(BLOCKS):
        weighed(last, last % 2, i)

    def give(by, near=False):
        b = lax.rem(st + by, 4)
        to = device(x, y, core * 2 + lax.div(b, 2), lax.rem(b, 2))
        if near:
            return pltpu.make_async_copy(o_out.at[by], o_in.at[z], o_recv.at[z])
        return pltpu.make_async_remote_copy(
            src_ref=o_out.at[by], dst_ref=o_in.at[z], send_sem=o_send.at[by],
            recv_sem=o_recv.at[z], device_id=to, device_id_type=MESH,
        )

    for by in (2, 1, 3, 0):
        b = lax.rem(st + by, 4)
        block = accum[rank_of(b)]
        heads = (block[:, :HEAD] / block[:, HEAD:]).astype(jnp.bfloat16)
        for g in range(GROUP):
            o_out[by, :, g * HEAD:(g + 1) * HEAD] = heads[g * TOKENS:(g + 1) * TOKENS]
        if by == 0:
            @pl.when(stays)
            def _():
                give(0, True).start()

            @pl.when(jnp.logical_not(stays))
            def _():
                give(0).start()
        else:
            give(by).start()

    for what in range(3):
        for by in (1, 2, 3):
            spread(by, what).wait_send()

        @pl.when(jnp.logical_not(stays))
        def _(what=what):
            spread(0, what).wait_send()
    gone = first_copies(0) + first_copies(1) + first_forwards()
    for p in range(4):
        gone += second_copies(p, 0) + second_copies(p, 1) + second_forwards(p)
        gone += [share("o%d%d" % (p, s)) for s in range(4)]
    for copy in gone:
        copy.wait_send()

    for fetch in fetches:
        fetch.wait()
    squares = jnp.zeros((TOKENS, 1), jnp.float32)
    tile = 512
    for number, by in enumerate((0, 1, 3, 2)):
        h = lax.rem(z + by, 4)
        pltpu.make_async_copy(o_in.at[h], o_in.at[h], o_recv.at[h]).wait()
        attended = o_in[h]
        rows = pl.ds(pl.multiple_of(h * WIDE, WIDE), WIDE)
        for n in range(D // tile):
            cols = slice(n * tile, (n + 1) * tile)
            part = jnp.dot(attended, w_v[rows, cols], preferred_element_type=jnp.float32)
            if number > 0:
                part = part + proj[:, cols]
            proj[:, cols] = part
            if number == 3:
                squares = squares + jnp.sum(part * part, axis=1, keepdims=True)
    inverse = lax.rsqrt(squares * (1.0 / D) + 1e-06)
    gate = gate_v[pl.ds(noise_ref[0], 1), :] * gain_ref[...]

    def result(n):
        cols = slice(n * tile, (n + 1) * tile)
        return pltpu.make_async_copy(mixed.at[:, cols], out_hbm.at[0, :, cols], out_sem.at[n])

    for n in range(D // tile):
        cols = slice(n * tile, (n + 1) * tile)
        mixed[:, cols] = (
            states_v[0, :, cols].astype(jnp.float32) + proj[:, cols] * inverse * gate[:, cols]
        ).astype(jnp.bfloat16)
        result(n).start()

    for by in (1, 2, 3):
        give(by).wait_send()

    @pl.when(jnp.logical_not(stays))
    def _():
        give(0).wait_send()

    for n in range(D // tile):
        result(n).wait()


def local(
    states, queries, keys, values, out_weight, norm_gain, gate_table, noise_steps, block_order
):
    hbm = pl.BlockSpec(memory_space=pl.ANY)
    smem = pl.BlockSpec(memory_space=pltpu.SMEM)
    vmem = pl.BlockSpec(memory_space=pltpu.VMEM)
    bf16, f32 = jnp.bfloat16, jnp.float32
    dma = pltpu.SemaphoreType.DMA
    return pl.pallas_call(
        kernel,
        out_shape=jax.ShapeDtypeStruct((1, TOKENS, D), bf16),
        in_specs=[smem, smem, hbm, hbm, hbm, hbm, hbm, vmem, hbm],
        out_specs=hbm,
        scratch_shapes=[
            pltpu.VMEM((BLOCKS, TOKENS, WIDE), bf16),
            pltpu.VMEM((BLOCKS, TOKENS, HEAD), bf16),
            pltpu.VMEM((BLOCKS, TOKENS, HEAD), bf16),
            pltpu.VMEM((QROWS, 2 * HEAD), bf16),
            pltpu.VMEM((32, 2, BLOCKS, TOKENS, HEAD), bf16),
            pltpu.VMEM((2, BLOCKS, QROWS, STEP_ROWS), f32),
            pltpu.VMEM((QROWS, HEAD), f32),
            pltpu.VMEM((BLOCKS, WIDE, 2 * HEAD), f32),
            pltpu.VMEM((BLOCKS, TOKENS, WIDE), bf16),
            pltpu.VMEM((KV_HEADS, TOKENS, WIDE), bf16),
            pltpu.VMEM((KV_HEADS * WIDE, D), bf16),
            pltpu.VMEM((1, TOKENS, D), bf16),
            pltpu.VMEM(gate_table.shape, f32),
            pltpu.VMEM((TOKENS, D), f32),
            pltpu.VMEM((TOKENS, D), bf16),
            dma((3, 4)), dma((3, 4)), dma((16, 2)), dma((16,)), dma((30,)), dma((16,)),
            dma((4,)), dma((4,)), dma((3,)), dma((6,)),
        ],
        compiler_params=pltpu.CompilerParams(
            collective_id=0, has_side_effects=True, vmem_limit_bytes=56 * 2**20
        ),
        cost_estimate=pl.CostEstimate(
            flops=9_300_000_000, bytes_accessed=20_000_000, transcendentals=16_000_000
        ),
        name="attend",
    )(
        block_order, noise_steps, queries, keys, values, states, out_weight,
        norm_gain.reshape(1, D), gate_table,
    )


def solution(mesh):
    placed = (
        P("stretch", "mp", None),
        P("stretch", "mp", None),
        P("stretch", "mp", None),
        P("stretch", "mp", None),
        P(),
        P(),
        P(),
        P("stretch"),
        P(),
    )
    return jax.shard_map(
        local, mesh=mesh, in_specs=placed, out_specs=P("stretch", "mp", None), check_vma=False
    )
```

```python
import functools
import math

import jax
import jax.numpy as jnp
from jax import lax
from jax.experimental import pallas as pl
from jax.experimental.pallas import tpu as pltpu
from jax.sharding import PartitionSpec as P

HEAD = 128
KV_HEADS = 4
GROUP = 3
WIDE = GROUP * HEAD
TOKENS = 128
BLOCKS = 4
D = 3072
QROWS = BLOCKS * WIDE
SCALE = math.log2(math.e) / math.sqrt(HEAD)
MESH = pl.DeviceIdType.MESH
NT = (((1,), (1,)), ((), ()))

STEPS = (
    ("o00", "s00"),
    ("o20", "o10"),
    ("s10", "s20"),
    ("o02", "o01"),
    ("s02", "s01"),
    ("o12", "o11"),
    ("o30", "s12"),
    ("o03", "s11"),
    ("s30", "o22"),
    ("s21", "o21"),
    ("o32", "s03"),
    ("s31", "o31"),
    ("o23", "s22"),
    ("o13", "s32"),
    ("o33", "s13"),
    ("s23", "s33"),
)
SENDS = {
    1: ("o20", "o10", "S10", "S11", "f3"),
    3: ("o02", "o01", "F0"),
    4: ("S20", "S21"),
    5: ("o30",),
    6: ("S31", "S30"),
    8: ("o21", "F2"),
    9: ("F1",),
    10: ("o31", "F3"),
}
EARLY = (0, 2)
PLACE = {name: i for i, name in enumerate(n for step in STEPS for n in step)}
HALVES = 2
STEP_ROWS = HALVES * TOKENS
FETCH_STEPS = range(2, 2 + KV_HEADS * GROUP)


def unit_number(name):
    return int(name[1]) * 4 + int(name[2])


def needed(op):
    if op == "f3":
        return ("o10", "o20")
    if op[0] == "S":
        return ("o%s0" % op[1],)
    if op[0] == "F":
        return ("o%s1" % op[1], "o%s2" % op[1])
    return (op,)


def plan():
    taken, steps = {"o00"}, []
    for number, names in enumerate(STEPS):
        todo = []
        for op in SENDS.get(number, ()) + names:
            for name in needed(op):
                if name not in taken:
                    taken.add(name)
                    todo.append(name)
            if op[0] in "fSF":
                todo.append(op)
        steps.append(tuple(todo))
    return steps


def kernel(
    order_ref, noise_ref, q_hbm, k_hbm, v_hbm, states_hbm, w_hbm, gain_ref, gate_hbm,
    out_hbm,
    q_in, k_in, v_in, q_two, kv, scores, top, accum, o_out, o_in, w_v, states_v, gate_v, proj, mixed,
    qkv_send, qkv_recv, own_recv, sib_recv, own_send, sib_send, o_send, o_recv, fetch_sem, out_sem,
):
    st = lax.axis_index("stretch")
    mp = lax.axis_index("mp")
    core = lax.rem(st, 2)
    z_hi = lax.rem(mp, 2)
    z = z_hi * 2 + lax.div(st, 2)
    y = lax.rem(lax.div(mp, 2), 4)
    x = lax.div(mp, 8)

    def device(xx, yy, zz, cc):
        return (lax.rem(zz, 2) * 2 + cc, xx * 8 + yy * 2 + lax.div(zz, 2))

    def ring(axis_is_x, by):
        return device(
            lax.rem(x + by * axis_is_x, 4), lax.rem(y + by * (1 - axis_is_x), 4), z, core
        )

    first_is_x = 1 - core
    first_plus, first_minus = ring(first_is_x, 1), ring(first_is_x, 3)
    second_plus, second_minus = ring(core, 1), ring(core, 3)
    sibling = device(x, y, z, 1 - core)

    barrier = pltpu.get_barrier_semaphore()
    for by in range(1, 8):
        other = lax.rem(z * 2 + core + by, 8)
        pl.semaphore_signal(
            barrier, inc=1, device_id=device(x, y, lax.div(other, 2), lax.rem(other, 2)),
            device_id_type=MESH,
        )
    for neighbour in (first_plus, first_minus, second_plus, second_minus):
        pl.semaphore_signal(barrier, inc=1, device_id=neighbour, device_id_type=MESH)
    pl.semaphore_wait(barrier, 11)

    def spread(by, what, near=False):
        h = lax.rem(z + by, 4)
        source, target, width = ((k_hbm, k_in, HEAD), (v_hbm, v_in, HEAD), (q_hbm, q_in, WIDE))[what]
        src = source.at[0, :, pl.ds(pl.multiple_of(h * width, width), width)]
        if near:
            return pltpu.make_async_copy(src, target.at[st], qkv_recv.at[what, st])
        return pltpu.make_async_remote_copy(
            src_ref=src, dst_ref=target.at[st], send_sem=qkv_send.at[what, by],
            recv_sem=qkv_recv.at[what, st], device_id=device(x, y, h, z_hi), device_id_type=MESH,
        )

    stays = core == z_hi
    for what in range(3):
        for by in (2, 1, 3):
            spread(by, what).start()

        @pl.when(stays)
        def _(what=what):
            spread(0, what, True).start()

        @pl.when(jnp.logical_not(stays))
        def _(what=what):
            spread(0, what).start()

    def weights(number):
        rows = slice(number * TOKENS, (number + 1) * TOKENS)
        return pltpu.make_async_copy(w_hbm.at[rows], w_v.at[rows], fetch_sem.at[0])

    fetches = [
        pltpu.make_async_copy(gate_hbm, gate_v, fetch_sem.at[1]),
        pltpu.make_async_copy(states_hbm, states_v, fetch_sem.at[2]),
        pltpu.make_async_copy(w_hbm, w_v, fetch_sem.at[0]),
    ]

    def rank_of(b):
        rank, place = jnp.int32(0), order_ref[b]
        for c in range(BLOCKS):
            other = order_ref[c]
            before = (other < place) | ((other == place) & (c < b))
            rank = rank + jnp.where(before, 1, 0)
        return rank

    ranks = [rank_of(jnp.int32(b)) for b in range(BLOCKS)]
    placed = []
    for i in range(BLOCKS):
        at = jnp.int32(0)
        for b in range(BLOCKS):
            at = at + jnp.where(ranks[b] == i, b, 0)
        placed.append(at)

    def landed(what):
        target = (k_in, v_in, q_in)[what]
        for b in range(BLOCKS):
            pltpu.make_async_copy(target.at[b], target.at[b], qkv_recv.at[what, b]).wait()

    def unit(name):
        return kv.at[PLACE[name]]

    def send(number, source, target, sem, to, part=None):
        src, dst = unit(source), unit(target)
        if part is not None:
            src, dst = src.at[part], dst.at[part]
        return pltpu.make_async_remote_copy(
            src_ref=src, dst_ref=dst, send_sem=own_send.at[number], recv_sem=sem,
            device_id=to, device_id_type=MESH,
        )

    def recv_sem(name, part=0):
        return own_recv.at[unit_number(name), part]

    def first_copies(part):
        return [
            send(part * 2, "o00", "o10", recv_sem("o10", part), first_plus, part),
            send(part * 2 + 1, "o00", "o20", recv_sem("o20", part), first_minus, part),
        ]

    def first_forwards():
        return [
            send(4, "o10", "o30", recv_sem("o30", 0), first_plus, 0),
            send(5, "o20", "o30", recv_sem("o30", 1), first_minus, 1),
        ]

    def second_copies(p, part):
        here, at = "o%d0" % p, 6 + p * 6 + part * 2
        plus, minus = "o%d1" % p, "o%d2" % p
        return [
            send(at, here, plus, recv_sem(plus, part), second_plus, part),
            send(at + 1, here, minus, recv_sem(minus, part), second_minus, part),
        ]

    def second_forwards(p):
        far, at = "o%d3" % p, 10 + p * 6
        return [
            send(at, "o%d1" % p, far, recv_sem(far, 0), second_plus, 0),
            send(at + 1, "o%d2" % p, far, recv_sem(far, 1), second_minus, 1),
        ]

    def share(name):
        number = unit_number(name)
        return pltpu.make_async_remote_copy(
            src_ref=unit(name), dst_ref=unit("s" + name[1:]), send_sem=sib_send.at[number],
            recv_sem=sib_recv.at[number], device_id=sibling, device_id_type=MESH,
        )

    def begin(copies):
        for copy in copies:
            copy.start()

    def act(op):
        if op == "f3":
            begin(first_forwards())
        elif op[0] == "S":
            begin(second_copies(int(op[1]), int(op[2])))
        elif op[0] == "F":
            begin(second_forwards(int(op[1])))
        elif op[0] == "s":
            pltpu.make_async_copy(unit(op), unit(op), sib_recv.at[unit_number(op)]).wait()
        else:
            for part in range(2):
                here = unit(op).at[part]
                pltpu.make_async_copy(here, here, recv_sem(op, part)).wait()
            share(op).start()

    accum[...] = jnp.zeros_like(accum)
    top[...] = jnp.full_like(top, -1e30)

    mine = PLACE["o00"]
    for part, source in ((0, k_in), (1, v_in)):
        landed(part)
        for i in range(BLOCKS):
            kv[mine, part, i] = source[placed[i]]
        begin(first_copies(part))
    share("o00").start()

    landed(2)
    begin(second_copies(0, 0) + second_copies(0, 1))
    for i in range(BLOCKS):
        rows = q_in[placed[i]].astype(jnp.float32) * SCALE
        high = rows.astype(jnp.bfloat16)
        low = (rows - high.astype(jnp.float32)).astype(jnp.bfloat16)
        for g in range(GROUP):
            at = i * WIDE + g * HEAD
            q_two[at:at + TOKENS, 0:HEAD] = high[:, g * HEAD:(g + 1) * HEAD]
            q_two[at:at + TOKENS, HEAD:2 * HEAD] = low[:, g * HEAD:(g + 1) * HEAD]

    plans = plan()

    def events(number):
        for op in plans[number]:
            act(op)
        if number in FETCH_STEPS:
            weights(number - FETCH_STEPS[0]).start()
        if number == FETCH_STEPS[0]:
            fetches[0].start()
            fetches[1].start()

    def scored(g, held, j):
        keys = jnp.concatenate([kv[g * HALVES + c, 0, j] for c in range(HALVES)], axis=0)
        scores[held, j, j * WIDE:QROWS] = lax.dot_general(
            q_two[j * WIDE:QROWS], jnp.concatenate([keys, keys], axis=1), NT,
            preferred_element_type=jnp.float32,
        )

    def weighed(g, held, i):
        rows = slice(i * WIDE, (i + 1) * WIDE)
        old = top[rows]
        most = old
        for j in range(i + 1):
            for t in range(HALVES):
                most = jnp.maximum(most, scores[held, j, rows, t * HEAD:(t + 1) * HEAD])
        new = jnp.broadcast_to(jnp.max(most, axis=1, keepdims=True), old.shape)
        top[rows] = new
        fade = jnp.exp2(old - new)
        total = accum[i] * jnp.concatenate([fade, fade], axis=1)
        shift = jnp.concatenate([new] * HALVES, axis=1)
        for j in range(i + 1):
            weights = jnp.exp2(scores[held, j, rows] - shift).astype(jnp.bfloat16)
            vals = jnp.concatenate([kv[g * HALVES + c, 1, j] for c in range(HALVES)], axis=0)
            vals = jnp.concatenate([vals, jnp.ones_like(vals)], axis=1)
            total = total + jnp.dot(weights, vals, preferred_element_type=jnp.float32)
        accum[i] = total

    def pair(g, held):
        for i in range(BLOCKS):
            scored(g + 1, 1 - held, i)
            weighed(g, held, i)

    last = len(STEPS) - 1
    events(0)
    for i in range(BLOCKS):
        scored(0, 0, i)

    for g in range(last):
        if g in EARLY:
            for i in range(BLOCKS):
                weighed(g, g % 2, i)
            events(g + 1)
            for i in range(BLOCKS):
                scored(g + 1, 1 - g % 2, i)
        else:
            events(g + 1)
            pair(g, g % 2)
    for i in range(BLOCKS):
        weighed(last, last % 2, i)

    def give(by, near=False):
        b = lax.rem(st + by, 4)
        to = device(x, y, core * 2 + lax.div(b, 2), lax.rem(b, 2))
        if near:
            return pltpu.make_async_copy(o_out.at[by], o_in.at[z], o_recv.at[z])
        return pltpu.make_async_remote_copy(
            src_ref=o_out.at[by], dst_ref=o_in.at[z], send_sem=o_send.at[by],
            recv_sem=o_recv.at[z], device_id=to, device_id_type=MESH,
        )

    for by in (2, 1, 3, 0):
        b = lax.rem(st + by, 4)
        block = accum[rank_of(b)]
        heads = (block[:, :HEAD] / block[:, HEAD:]).astype(jnp.bfloat16)
        for g in range(GROUP):
            o_out[by, :, g * HEAD:(g + 1) * HEAD] = heads[g * TOKENS:(g + 1) * TOKENS]
        if by == 0:
            @pl.when(stays)
            def _():
                give(0, True).start()

            @pl.when(jnp.logical_not(stays))
            def _():
                give(0).start()
        else:
            give(by).start()

    for what in range(3):
        for by in (1, 2, 3):
            spread(by, what).wait_send()

        @pl.when(jnp.logical_not(stays))
        def _(what=what):
            spread(0, what).wait_send()
    gone = first_copies(0) + first_copies(1) + first_forwards()
    for p in range(4):
        gone += second_copies(p, 0) + second_copies(p, 1) + second_forwards(p)
        gone += [share("o%d%d" % (p, s)) for s in range(4)]
    for copy in gone:
        copy.wait_send()

    for fetch in fetches:
        fetch.wait()
    squares = jnp.zeros((TOKENS, 1), jnp.float32)
    tile = 512
    for number, by in enumerate((0, 1, 3, 2)):
        h = lax.rem(z + by, 4)
        pltpu.make_async_copy(o_in.at[h], o_in.at[h], o_recv.at[h]).wait()
        attended = o_in[h]
        rows = pl.ds(pl.multiple_of(h * WIDE, WIDE), WIDE)
        for n in range(D // tile):
            cols = slice(n * tile, (n + 1) * tile)
            part = jnp.dot(attended, w_v[rows, cols], preferred_element_type=jnp.float32)
            if number > 0:
                part = part + proj[:, cols]
            proj[:, cols] = part
            if number == 3:
                squares = squares + jnp.sum(part * part, axis=1, keepdims=True)
    inverse = lax.rsqrt(squares * (1.0 / D) + 1e-06)
    gate = gate_v[pl.ds(noise_ref[0], 1), :] * gain_ref[...]

    def result(n):
        cols = slice(n * tile, (n + 1) * tile)
        return pltpu.make_async_copy(mixed.at[:, cols], out_hbm.at[0, :, cols], out_sem.at[n])

    for n in range(D // tile):
        cols = slice(n * tile, (n + 1) * tile)
        mixed[:, cols] = (
            states_v[0, :, cols].astype(jnp.float32) + proj[:, cols] * inverse * gate[:, cols]
        ).astype(jnp.bfloat16)
        result(n).start()

    for by in (1, 2, 3):
        give(by).wait_send()

    @pl.when(jnp.logical_not(stays))
    def _():
        give(0).wait_send()

    for n in range(D // tile):
        result(n).wait()


def local(
    states, queries, keys, values, out_weight, norm_gain, gate_table, noise_steps, block_order
):
    hbm = pl.BlockSpec(memory_space=pl.ANY)
    smem = pl.BlockSpec(memory_space=pltpu.SMEM)
    vmem = pl.BlockSpec(memory_space=pltpu.VMEM)
    bf16, f32 = jnp.bfloat16, jnp.float32
    dma = pltpu.SemaphoreType.DMA
    return pl.pallas_call(
        kernel,
        out_shape=jax.ShapeDtypeStruct((1, TOKENS, D), bf16),
        in_specs=[smem, smem, hbm, hbm, hbm, hbm, hbm, vmem, hbm],
        out_specs=hbm,
        scratch_shapes=[
            pltpu.VMEM((BLOCKS, TOKENS, WIDE), bf16),
            pltpu.VMEM((BLOCKS, TOKENS, HEAD), bf16),
            pltpu.VMEM((BLOCKS, TOKENS, HEAD), bf16),
            pltpu.VMEM((QROWS, 2 * HEAD), bf16),
            pltpu.VMEM((32, 2, BLOCKS, TOKENS, HEAD), bf16),
            pltpu.VMEM((2, BLOCKS, QROWS, STEP_ROWS), f32),
            pltpu.VMEM((QROWS, HEAD), f32),
            pltpu.VMEM((BLOCKS, WIDE, 2 * HEAD), f32),
            pltpu.VMEM((BLOCKS, TOKENS, WIDE), bf16),
            pltpu.VMEM((KV_HEADS, TOKENS, WIDE), bf16),
            pltpu.VMEM((KV_HEADS * WIDE, D), bf16),
            pltpu.VMEM((1, TOKENS, D), bf16),
            pltpu.VMEM(gate_table.shape, f32),
            pltpu.VMEM((TOKENS, D), f32),
            pltpu.VMEM((TOKENS, D), bf16),
            dma((3, 4)), dma((3, 4)), dma((16, 2)), dma((16,)), dma((30,)), dma((16,)),
            dma((4,)), dma((4,)), dma((3,)), dma((6,)),
        ],
        compiler_params=pltpu.CompilerParams(
            collective_id=0, has_side_effects=True, vmem_limit_bytes=56 * 2**20
        ),
        cost_estimate=pl.CostEstimate(
            flops=9_300_000_000, bytes_accessed=20_000_000, transcendentals=16_000_000
        ),
        name="attend",
    )(
        block_order, noise_steps, queries, keys, values, states, out_weight,
        norm_gain.reshape(1, D), gate_table,
    )


def solution(mesh):
    placed = (
        P("stretch", "mp", None),
        P("stretch", "mp", None),
        P("stretch", "mp", None),
        P("stretch", "mp", None),
        P(),
        P(),
        P(),
        P("stretch"),
        P(),
    )
    return jax.shard_map(
        local, mesh=mesh, in_specs=placed, out_specs=P("stretch", "mp", None), check_vma=False
    )
```
